256 devices in a mesh: blk: 64 (over z, x_hi, y), ch: 4 (over x_lo, core).
Axes of the slice: x: 4 (x_hi: 2, x_lo: 2; x = x_hi * 2 + x_lo), y: 4, z: 8, core: 2. Of those that a mesh axis runs over, the one named last changes fastest.
Arguments:
- features: bfloat16 [49152, 512], P('blk', 'ch'), may hold values from -6 to 6
- tile_values: bfloat16 [8192, 128, 128], P('blk'), may hold values from -600 to 600
- tile_source: int32 [8192], P('blk'), may hold values from 0 to 384, as said below
- tile_target: int32 [8192], P('blk'), may hold values from 0 to 5
- tile_count: int32 [64], P('blk'), may hold values from 32 to 128
- weights: bfloat16 [3, 512, 512], replicated, may hold values from -0.15625 to 0.15625
- bias_vector: float32 [512], replicated, may hold values from -3 to 3
Outputs:
- mixed: bfloat16 [49152, 512], P('blk', 'ch')
The draws below stay inside these ranges and needn't reach their ends.
Inputs may be any that keep to these rules, and one draw needn't show every extreme that they name: `tile_source`: in each index of blk the live slots come first, sorted by value, and at most 4 of them name row tiles of one index of blk (tiles 6 * b to 6 * b + 5), a bound that every index of blk reaches; slots from tile_count on hold 384.
All inputs are finite; a program needn't handle non-finite values.
Results may differ from the reference program's by a relative error of at most 0.01.
Values may be sent and summed in bfloat16 or wider, within the bound.
No kernel may reach another device: no remote copies, remote signals or barrier semaphores. Data moves between devices by JAX's collectives and lax.ppermute only.
A program may use at most 64 MiB of HBM per device.

```python
import math
import jax
import jax.numpy as jnp
from jax import lax

CHANNELS = 512
TILE = 128
RT_DEV = 6
TILES_DEV = 128
ROWS_DEV = 768
SCAP = 4
GATES = 49152
N_BLK = 64


def pattern(key):
    base_key = jax.random.fold_in(key, 11)
    full_dev = jax.random.randint(jax.random.fold_in(base_key, 1), (), 0, N_BLK)
    low_dev = (full_dev + 1 + jax.random.randint(jax.random.fold_in(base_key, 2), (), 0, N_BLK - 1)) % N_BLK

    def per_device(device):
        device_key = jax.random.fold_in(base_key, 100 + device)
        shuffled = jax.random.permutation(jax.random.fold_in(device_key, 1), (N_BLK - 1) * SCAP).astype(jnp.int32)
        lead_block = jax.random.randint(jax.random.fold_in(device_key, 2), (), 0, N_BLK).astype(jnp.int32)
        others = shuffled[:TILES_DEV - SCAP] // SCAP
        others = others + (others >= lead_block).astype(jnp.int32)
        blocks = jnp.concatenate([jnp.full((SCAP,), lead_block, jnp.int32), others])
        within = jax.random.randint(jax.random.fold_in(device_key, 3), (TILES_DEV,), 0, RT_DEV).astype(jnp.int32)
        halving = jax.random.randint(jax.random.fold_in(device_key, 4), (), 0, 2).astype(jnp.int32)
        live_count = jnp.right_shift(jnp.int32(TILES_DEV), halving)
        live_count = jnp.where(device == full_dev, TILES_DEV, jnp.where(device == low_dev, TILES_DEV // 4, live_count)).astype(jnp.int32)
        usable = jnp.arange(TILES_DEV, dtype=jnp.int32) < live_count
        sort_keys = jnp.where(usable, blocks * RT_DEV + within, N_BLK * RT_DEV).astype(jnp.int32)
        return (jnp.sort(sort_keys), live_count)
    sources, counts = jax.vmap(per_device)(jnp.arange(N_BLK, dtype=jnp.int32))
    return (sources.reshape(-1).astype(jnp.int32), counts.astype(jnp.int32))


def draw_tile_source(key, part):
    return pattern(key)[0]


def draw_tile_count(key, part):
    return pattern(key)[1]


def draw_tile_values(key, part):
    shape = (N_BLK * TILES_DEV, TILE, TILE)
    base_part = jnp.clip(jax.random.normal(jax.random.fold_in(key, 1), shape, jnp.float32), -6.0, 6.0)
    log_top = math.log(10.0)
    row_scale = jnp.exp(jax.random.uniform(jax.random.fold_in(key, 2), (N_BLK * TILES_DEV, TILE, 1), jnp.float32, 0.0, log_top))
    col_scale = jnp.exp(jax.random.uniform(jax.random.fold_in(key, 3), (N_BLK * TILES_DEV, 1, TILE), jnp.float32, 0.0, log_top))
    return jnp.clip(base_part * row_scale * col_scale, -600.0, 600.0).astype(jnp.bfloat16)


def place_ends(array, key, least, largest):
    longest = array.shape.index(max(array.shape))
    spots = []
    for shift in (0, 1):
        where = [jax.random.randint(jax.random.fold_in(key, axis), (), 0, length) for axis, length in enumerate(array.shape)]
        where[longest] = (where[longest] + shift) % array.shape[longest]
        spots.append(tuple(where))
    return array.at[spots[0]].set(least).at[spots[1]].set(largest)


def levels(own_key, extent, pieces, smallest, top_value):
    gain = 1.0
    for axis_at, blocks in pieces:
        draws = jax.random.uniform(jax.random.fold_in(jax.random.fold_in(own_key, 6), axis_at), (blocks,), jnp.float32, smallest / len(pieces), top_value / len(pieces))
        gain = gain * jnp.repeat(jnp.exp(draws), extent[axis_at] // blocks).reshape((-1,) + (1,) * (len(extent) - 1 - axis_at))
    return gain


def scatter_about(key, extent, scale, limit, shards=(), kind=jnp.bfloat16):
    entries = jax.random.normal(key, extent, jnp.float32) * scale
    if len(shards) > 0:
        entries = levels(key, extent, shards, -0.22, 0.18) * entries
    return jnp.clip(entries, min=-limit, max=limit).astype(kind)


def setup_inputs(seed: int = 0) -> dict:
    keys = jax.random.split(jax.random.key(seed), 8)
    return {
        "features": scatter_about(keys[0], (GATES, CHANNELS), 1.0, 6.0, ((0, 64), (1, 4))),
        "tile_values": draw_tile_values(jax.random.fold_in(keys[7], 71), 0),
        "tile_source": draw_tile_source(jax.random.fold_in(keys[7], 71), 0),
        "tile_target": place_ends(jax.random.randint(keys[3], (N_BLK * TILES_DEV,), 0, RT_DEV), jax.random.fold_in(keys[3], 1), 0, RT_DEV - 1).astype(jnp.int32),
        "tile_count": draw_tile_count(jax.random.fold_in(keys[7], 71), 0),
        "weights": scatter_about(keys[5], (3, CHANNELS, CHANNELS), (3 * CHANNELS) ** -0.5, 0.15625),
        "bias_vector": scatter_about(keys[6], (CHANNELS,), 0.5, 3.0, (), jnp.float32),
    }


def propagate(signal, tile_values, tile_source, tile_target, tile_count):
    blocks = signal.reshape(N_BLK * RT_DEV, TILE, CHANNELS)

    def per_device(device):
        first_tile = (device * TILES_DEV).astype(jnp.int32)
        values = lax.dynamic_slice_in_dim(tile_values, first_tile, TILES_DEV, 0).astype(jnp.float32)
        source = lax.dynamic_slice_in_dim(tile_source, first_tile, TILES_DEV, 0)
        target = lax.dynamic_slice_in_dim(tile_target, first_tile, TILES_DEV, 0)
        usable = jnp.arange(TILES_DEV, dtype=jnp.int32) < tile_count[device]
        picked = blocks[jnp.where(usable, source, 0)].astype(jnp.float32)
        product = jnp.einsum('tij,tjc->tic', values, picked, precision=lax.Precision.HIGHEST)
        product = jnp.where(usable[:, None, None], product, jnp.float32(0.0))
        running = jnp.zeros((RT_DEV, TILE, CHANNELS), jnp.float32).at[target].add(product)
        squares = jnp.where(usable[:, None], lax.optimization_barrier(jnp.sum(values * values, axis=2)), jnp.float32(0.0))
        row_norm = jnp.zeros((RT_DEV, TILE), jnp.float32).at[target].add(squares)
        return running * lax.rsqrt(1.0 + row_norm)[:, :, None]
    stacked_out = lax.map(per_device, jnp.arange(N_BLK, dtype=jnp.int32))
    return stacked_out.reshape(N_BLK * ROWS_DEV, CHANNELS)

def reference(features, tile_values, tile_source, tile_target, tile_count, weights, bias_vector):
    first_order = propagate(features, tile_values, tile_source, tile_target, tile_count).astype(jnp.bfloat16)
    second = propagate(first_order, tile_values, tile_source, tile_target, tile_count)
    second_order = (2.0 * second - features.astype(jnp.float32)).astype(jnp.bfloat16)
    result = jnp.dot(features, weights[0], preferred_element_type=jnp.float32)
    result = result + jnp.dot(first_order, weights[1], preferred_element_type=jnp.float32)
    result = result + jnp.dot(second_order, weights[2], preferred_element_type=jnp.float32)
    return (result + bias_vector[None, :]).astype(jnp.bfloat16)
```

```python
import jax
import jax.numpy as jnp
from jax import lax
from jax.experimental import pallas as pl
from jax.experimental.pallas import tpu as pltpu
from jax.sharding import PartitionSpec as P

NZ, NX, NY = 8, 2, 4
T = 128
RT = 6
ROWS = RT * T
HALF = 64
SLOTS = 128
RA = ROWS // 2
N_ACC = 4 * RT + 1
DUMMY = 4 * RT


def blk_id(z, x, y):
    return ((z % NZ) * NX + x % NX) * NY + y % NY


def shift(v, dz, dy):
    pairs = [
        (blk_id(z, x, y), blk_id(z + dz, x, y + dy))
        for z in range(NZ)
        for x in range(NX)
        for y in range(NY)
    ]
    return lax.ppermute(v, "blk", pairs)


def line_swap(v, flip_hi, flip_lo, flip_core):
    pairs = []
    for z in range(NZ):
        for xh in range(2):
            for y in range(NY):
                for xl in range(2):
                    for core in range(2):
                        src = blk_id(z, xh, y) * 4 + xl * 2 + core
                        dst = blk_id(z, xh ^ flip_hi, y) * 4 + (xl ^ flip_lo) * 2 + (core ^ flip_core)
                        pairs.append((src, dst))
    return lax.ppermute(v, ("blk", "ch"), pairs)


def ring_y(v):
    h = v.shape[0] // 2
    up, down = shift(v, 0, 1), shift(v, 0, -1)
    return [up, down, shift(up[:h], 0, 1), shift(down[h:], 0, -1)]


def ring_z(v):
    h = v.shape[0] // 2
    ups, downs = [], []
    up = down = v
    for _ in range(3):
        up, down = shift(up, 1, 0), shift(down, -1, 0)
        ups.append(up)
        downs.append(down)
    return ups + downs + [shift(up[:h], 1, 0), shift(down[h:], -1, 0)]


def gather_zy(v):
    first, second = v[:RA], v[RA:]
    a4 = jnp.concatenate([first] + ring_y(first), axis=0)
    b8 = jnp.concatenate([second] + ring_z(second), axis=0)
    return [a4] + ring_z(a4) + [b8] + ring_y(b8)


def source_rows(tile, z, y):
    block, part = tile // RT, tile % RT
    dz = (block // (NX * NY) - z) % NZ
    dy = (block % NY - y) % NY
    j = jnp.where(dz == 0, 0, jnp.where(dz == 4, 7, jnp.where(dz > 4, 8 - dz, dz + 3)))
    q = jnp.where(dy == 0, 0, jnp.where(dy == 3, 1, jnp.where(dy == 1, 2, 3)))
    in_a = (j * NY + q) * RA + part * T
    in_b = NZ * NY * RA + (q * NZ + j) * RA + (part - RT // 2) * T
    return jnp.where(part < RT // 2, in_a, in_b)


def mix_kernel(f0, f1, f2, f3, g0, g1, w_ref, b_ref, u0_ref, u1_ref, u2_ref):
    for r in range(RT):
        rows = slice(r * T, (r + 1) * T)
        parts = [f0[rows], f1[rows], f2[rows], f3[rows], g0[rows]]
        parts += [g1[k * ROWS + r * T : k * ROWS + (r + 1) * T] for k in range(3)]
        u = jnp.dot(jnp.concatenate(parts, axis=1), w_ref[...], preferred_element_type=jnp.float32)
        u2 = u[:, 2 * T :]
        u0_ref[rows] = u[:, :T] - u2 + b_ref[...]
        u1_ref[rows] = u[:, T : 2 * T]
        u2_ref[rows] = u2.astype(jnp.bfloat16)


def mix(pieces, w_all, bias_pair):
    n = ROWS * T
    return pl.pallas_call(
        mix_kernel,
        out_shape=[
            jax.ShapeDtypeStruct((ROWS, T), jnp.float32),
            jax.ShapeDtypeStruct((ROWS, T), jnp.float32),
            jax.ShapeDtypeStruct((ROWS, T), jnp.bfloat16),
        ],
        compiler_params=pltpu.CompilerParams(vmem_limit_bytes=16 * 2**20),
        cost_estimate=pl.CostEstimate(
            flops=2 * ROWS * 1024 * 384, bytes_accessed=n * 26 + 1024 * 384 * 2, transcendentals=0
        ),
        name="mix",
    )(*pieces, w_all, bias_pair)


def make_prop(scale, out_dtype, steps=8):
    own_n, sub_n = SLOTS // steps, SLOTS // (2 * steps)

    def kernel(meta, *refs):
        pieces = refs[:14]
        own, rec, swp, inv, base, out, x_all, acc, sems = refs[14:]
        step = pl.program_id(0)

        @pl.when(step == 0)
        def _():
            copies, at = [], 0
            for k, piece in enumerate(pieces):
                n = piece.shape[0]
                copies.append(pltpu.make_async_copy(piece, x_all.at[pl.ds(at, n)], sems.at[k]))
                at += n
            for c in copies:
                c.start()
            acc[...] = jnp.zeros_like(acc)
            for c in copies:
                c.wait()

        def group(ref, first, base_slot):
            prods = []
            for k in range(4):
                off = pl.multiple_of(meta[base_slot + k], T)
                prods.append(
                    jnp.dot(ref[first + k], x_all[pl.ds(off, T), :], preferred_element_type=jnp.float32)
                )
            for k in range(4):
                slot = meta[2 * SLOTS + base_slot + k]
                acc[slot] += prods[k]

        for ref, n, start in ((own, own_n, 0), (rec, sub_n, SLOTS), (swp, sub_n, SLOTS + SLOTS // 2)):
            for first in range(0, n, 4):
                base_slot = start + step * n + first

                @pl.when(meta[2 * SLOTS + base_slot] != DUMMY)
                def _(ref=ref, first=first, base_slot=base_slot):
                    group(ref, first, base_slot)

        @pl.when(step == steps - 1)
        def _():
            low = lax.broadcasted_iota(jnp.int32, (T, T), 1) < HALF
            for r in range(RT):
                rows = slice(r * T, (r + 1) * T)
                straight = jnp.where(low, acc[r], acc[3 * RT + r])
                crossed = jnp.where(low, acc[2 * RT + r], acc[RT + r])
                total = straight + pltpu.roll(crossed, HALF, 1)
                out[rows] = (base[rows] + scale * (inv[rows] * total)).astype(out_dtype)

    def call(meta, pieces, own, rec, swp, inv, base):
        return pl.pallas_call(
            kernel,
            grid_spec=pltpu.PrefetchScalarGridSpec(
                num_scalar_prefetch=1,
                grid=(steps,),
                in_specs=[pl.BlockSpec(memory_space=pl.ANY)] * 14
                + [
                    pl.BlockSpec((own_n, T, T), lambda i, m: (i, 0, 0)),
                    pl.BlockSpec((sub_n, T, T), lambda i, m: (i, 0, 0)),
                    pl.BlockSpec((sub_n, T, T), lambda i, m: (i, 0, 0)),
                    pl.BlockSpec((ROWS, T), lambda i, m: (0, 0)),
                    pl.BlockSpec((ROWS, T), lambda i, m: (0, 0)),
                ],
                out_specs=pl.BlockSpec((ROWS, T), lambda i, m: (0, 0)),
                scratch_shapes=[
                    pltpu.VMEM((NZ * NY * ROWS, T), jnp.bfloat16),
                    pltpu.VMEM((N_ACC, T, T), jnp.float32),
                    pltpu.SemaphoreType.DMA((14,)),
                ],
            ),
            out_shape=jax.ShapeDtypeStruct((ROWS, T), out_dtype),
            compiler_params=pltpu.CompilerParams(
                dimension_semantics=("arbitrary",), vmem_limit_bytes=24 * 2**20
            ),
            cost_estimate=pl.CostEstimate(
                flops=2 * 2 * SLOTS * T**3, bytes_accessed=16 * 2**20, transcendentals=0
            ),
            name="prop",
        )(meta, *pieces, own, rec, swp, inv, base)

    return call


def per_device(features, tile_values, tile_source, tile_target, tile_count, weights, bias_vector):
    blk, ch = lax.axis_index("blk"), lax.axis_index("ch")
    z, xh, y = blk // (NX * NY), (blk // NY) % NX, blk % NY
    xl, core = ch // 2, ch % 2

    swap_f = line_swap(features, 0, 0, 1)
    near = line_swap(features, 0, 1, 0)
    cross = line_swap(features, 1, 1, 0)
    over = line_swap(features, 1, 0, 0)
    swap_rest = line_swap(jnp.concatenate([near, cross, over], axis=0), 0, 0, 1)

    col = ch * T + xh * HALF
    w_cols = lax.dynamic_slice_in_dim(weights, col, HALF, 2)
    w_cols = w_cols.reshape(3, 4, T, HALF).transpose(1, 2, 0, 3)
    lane_half = jnp.arange(2, dtype=jnp.int32)[None, None, :, None]

    def piece_weights(lo, c, hi):
        w = lax.dynamic_index_in_dim(w_cols, lo * 2 + c, 0, keepdims=False)
        w = jnp.where(lane_half == hi, w[:, :, None, :], jnp.zeros((), w.dtype))
        return w.reshape(T, 3 * T)

    order = ((0, 0), (1, 0), (1, 1), (0, 1))
    w_all = jnp.concatenate(
        [piece_weights(xl ^ lo, core, xh ^ hi) for lo, hi in order]
        + [piece_weights(xl ^ lo, 1 - core, xh ^ hi) for lo, hi in order],
        axis=0,
    )
    bias_part = lax.dynamic_slice_in_dim(bias_vector, col, HALF, 0)
    bias_pair = jnp.concatenate([bias_part, bias_part])[None, :]

    usable = jnp.arange(SLOTS, dtype=jnp.int32) < tile_count[0]
    source = jnp.where(usable, tile_source, 0)
    offset = source_rows(source, z, y)
    source_hi = (source // (RT * NY)) % NX
    slot = jnp.where(usable, (xh * 2 + source_hi) * RT + tile_target, DUMMY)
    own_meta = jnp.stack([offset, slot]).astype(jnp.int32)
    far_meta = line_swap(own_meta, 1, 1, 0)
    far_meta = jnp.where(core == 0, far_meta, jnp.roll(far_meta, SLOTS // 2, axis=1))
    meta = jnp.concatenate([own_meta, far_meta], axis=1).reshape(-1)

    sent = lax.dynamic_slice_in_dim(tile_values, core * (SLOTS // 2), SLOTS // 2, 0)
    received = line_swap(sent, 1, 1, 0)
    swapped = line_swap(received, 0, 0, 1)

    squares = jnp.einsum(
        "tij,tij->ti", tile_values, tile_values, preferred_element_type=jnp.float32
    )
    squares = jnp.where(usable[:, None], squares, 0.0)
    onehot = (
        (tile_target[:, None] == jnp.arange(RT, dtype=jnp.int32)[None, :]) & usable[:, None]
    ).astype(jnp.float32)
    row_norm = jnp.dot(onehot.T, squares, precision=lax.Precision.HIGHEST)
    inverse = lax.rsqrt(1.0 + row_norm)
    far_inverse = line_swap(inverse, 1, 1, 0)
    lanes_hi = jnp.arange(T, dtype=jnp.int32)[None, :] // HALF
    inv_pair = jnp.where(
        lanes_hi == xh, inverse.reshape(-1)[:, None], far_inverse.reshape(-1)[:, None]
    )

    u0, u1, u2 = mix([features, near, cross, over, swap_f, swap_rest], w_all, bias_pair)
    v = make_prop(2.0, jnp.bfloat16)(meta, gather_zy(u2), tile_values, received, swapped, inv_pair, u1)
    w = make_prop(1.0, jnp.bfloat16)(meta, gather_zy(v), tile_values, received, swapped, inv_pair, u0)
    back = line_swap(w, 1, 0, 0)
    back = jnp.concatenate([back[:, HALF:], back[:, :HALF]], axis=1)
    return jnp.where(lanes_hi == xh, w, back)


def solution(mesh):
    return jax.shard_map(
        per_device,
        mesh=mesh,
        in_specs=(P("blk", "ch"), P("blk", None, None), P("blk"), P("blk"), P("blk"), P(), P()),
        out_specs=P("blk", "ch"),
        check_vma=False,
    )
```

```python
import jax
import jax.numpy as jnp
from jax import lax
from jax.experimental import pallas as pl
from jax.experimental.pallas import tpu as pltpu
from jax.sharding import PartitionSpec as P

NZ, NX, NY = 8, 2, 4
T = 128
RT = 6
ROWS = RT * T
HALF = 64
SLOTS = 128
RA = ROWS // 2
N_ACC = 4 * RT + 1
DUMMY = 4 * RT


def blk_id(z, x, y):
    return ((z % NZ) * NX + x % NX) * NY + y % NY


def shift(v, dz, dy):
    pairs = [
        (blk_id(z, x, y), blk_id(z + dz, x, y + dy))
        for z in range(NZ)
        for x in range(NX)
        for y in range(NY)
    ]
    return lax.ppermute(v, "blk", pairs)


def line_swap(v, flip_hi, flip_lo, flip_core):
    pairs = []
    for z in range(NZ):
        for xh in range(2):
            for y in range(NY):
                for xl in range(2):
                    for core in range(2):
                        src = blk_id(z, xh, y) * 4 + xl * 2 + core
                        dst = blk_id(z, xh ^ flip_hi, y) * 4 + (xl ^ flip_lo) * 2 + (core ^ flip_core)
                        pairs.append((src, dst))
    return lax.ppermute(v, ("blk", "ch"), pairs)


def ring_y(v):
    h = v.shape[0] // 2
    up, down = shift(v, 0, 1), shift(v, 0, -1)
    return [up, down, shift(up[:h], 0, 1), shift(down[h:], 0, -1)]


def ring_z(v):
    h = v.shape[0] // 2
    ups, downs = [], []
    up = down = v
    for _ in range(3):
        up, down = shift(up, 1, 0), shift(down, -1, 0)
        ups.append(up)
        downs.append(down)
    return ups + downs + [shift(up[:h], 1, 0), shift(down[h:], -1, 0)]


def gather_zy(v):
    first, second = v[:RA], v[RA:]
    near_y = ring_y(first)
    a4 = jnp.concatenate([first] + near_y, axis=0)
    b8 = jnp.concatenate([second] + ring_z(second), axis=0)
    return [a4] + ring_z(a4) + [b8] + ring_y(b8)


def after(v, event):
    return lax.optimization_barrier((v, event))[0]


def source_rows(tile, z, y):
    block, part = tile // RT, tile % RT
    dz = (block // (NX * NY) - z) % NZ
    dy = (block % NY - y) % NY
    j = jnp.where(dz == 0, 0, jnp.where(dz == 4, 7, jnp.where(dz > 4, 8 - dz, dz + 3)))
    q = jnp.where(dy == 0, 0, jnp.where(dy == 3, 1, jnp.where(dy == 1, 2, 3)))
    in_a = (j * NY + q) * RA + part * T
    in_b = NZ * NY * RA + (q * NZ + j) * RA + (part - RT // 2) * T
    return jnp.where(part < RT // 2, in_a, in_b)


def mix_kernel(place, f0, f1, f2, f3, g0, g1, w_ref, b_ref, u0_ref, u1_ref, u2_ref, w_cat):
    ch, xh = place[0], place[1]
    cols = pl.ds(pl.multiple_of(ch * T, T), T)
    for k in range(4):
        part = pl.ds(pl.multiple_of(place[2 + k] * T, T), T)
        for m in range(3):
            w_cat[k * T : (k + 1) * T, m * T : (m + 1) * T] = w_ref[m, part, cols]
    mine = lax.broadcasted_iota(jnp.int32, (T, T), 1) // HALF == xh
    bias = jnp.broadcast_to(b_ref[:, cols], (T, T))
    bias = jnp.where(mine, bias, pltpu.roll(bias, HALF, 1))
    for r in range(RT):
        rows = slice(r * T, (r + 1) * T)
        rest = [slice(k * ROWS + r * T, k * ROWS + (r + 1) * T) for k in range(3)]
        own = jnp.concatenate([f0[rows], f1[rows], g0[rows], g1[rest[0]]], axis=1)
        other = jnp.concatenate([f3[rows], f2[rows], g1[rest[2]], g1[rest[1]]], axis=1)
        u_own = jnp.dot(own, w_cat[...], preferred_element_type=jnp.float32)
        u_other = jnp.dot(other, w_cat[...], preferred_element_type=jnp.float32)
        u = [
            jnp.where(
                mine,
                u_own[:, m * T : (m + 1) * T],
                pltpu.roll(u_other[:, m * T : (m + 1) * T], HALF, 1),
            )
            for m in range(3)
        ]
        u0_ref[rows] = u[0] - u[2] + bias
        u1_ref[rows] = u[1]
        u2_ref[rows] = u[2].astype(jnp.bfloat16)


def mix(place, pieces, weights, bias):
    vmem = pl.BlockSpec(memory_space=pltpu.VMEM)
    return pl.pallas_call(
        mix_kernel,
        in_specs=[pl.BlockSpec(memory_space=pltpu.SMEM)] + [vmem] * 8,
        out_specs=[vmem] * 3,
        out_shape=[
            jax.ShapeDtypeStruct((ROWS, T), jnp.float32),
            jax.ShapeDtypeStruct((ROWS, T), jnp.float32),
            jax.ShapeDtypeStruct((ROWS, T), jnp.bfloat16),
        ],
        scratch_shapes=[pltpu.VMEM((4 * T, 3 * T), jnp.bfloat16)],
        compiler_params=pltpu.CompilerParams(vmem_limit_bytes=16 * 2**20),
        cost_estimate=pl.CostEstimate(
            flops=2 * ROWS * 1024 * 384, bytes_accessed=4 * 2**20, transcendentals=0
        ),
        name="mix",
    )(place, *pieces, weights, bias)


def make_prop(scale, out_dtype, steps=4):
    own_n, sub_n = SLOTS // steps, SLOTS // (2 * steps)

    def kernel(meta, *refs):
        pieces = refs[:14]
        own, rec, swp, inv, base, out, x_all, acc, sems = refs[14:]
        step = pl.program_id(0)

        @pl.when(step == 0)
        def _():
            copies, at = [], 0
            for k, piece in enumerate(pieces):
                n = piece.shape[0]
                copies.append(pltpu.make_async_copy(piece, x_all.at[pl.ds(at, n)], sems.at[k]))
                at += n
            for c in copies:
                c.start()
            acc[...] = jnp.zeros_like(acc)
            for c in copies:
                c.wait()

        for ref, n, start in ((own, own_n, 0), (rec, sub_n, SLOTS), (swp, sub_n, SLOTS + SLOTS // 2)):
            for k in range(n):
                at = start + step * n + k
                off = pl.multiple_of(meta[at], T)
                acc[meta[2 * SLOTS + at]] += jnp.dot(
                    ref[k], x_all[pl.ds(off, T), :], preferred_element_type=jnp.float32
                )

        @pl.when(step == steps - 1)
        def _():
            low = lax.broadcasted_iota(jnp.int32, (T, T), 1) < HALF
            for r in range(RT):
                rows = slice(r * T, (r + 1) * T)
                straight = jnp.where(low, acc[r], acc[3 * RT + r])
                crossed = jnp.where(low, acc[2 * RT + r], acc[RT + r])
                total = straight + pltpu.roll(crossed, HALF, 1)
                out[rows] = (base[rows] + scale * (inv[rows] * total)).astype(out_dtype)

    def call(meta, pieces, own, rec, swp, inv, base):
        return pl.pallas_call(
            kernel,
            grid_spec=pltpu.PrefetchScalarGridSpec(
                num_scalar_prefetch=1,
                grid=(steps,),
                in_specs=[pl.BlockSpec(memory_space=pl.ANY)] * 14
                + [
                    pl.BlockSpec((own_n, T, T), lambda i, m: (i, 0, 0)),
                    pl.BlockSpec((sub_n, T, T), lambda i, m: (i, 0, 0)),
                    pl.BlockSpec((sub_n, T, T), lambda i, m: (i, 0, 0)),
                    pl.BlockSpec((ROWS, T), lambda i, m: (0, 0)),
                    pl.BlockSpec((ROWS, T), lambda i, m: (0, 0)),
                ],
                out_specs=pl.BlockSpec((ROWS, T), lambda i, m: (0, 0)),
                scratch_shapes=[
                    pltpu.VMEM((NZ * NY * ROWS, T), jnp.bfloat16),
                    pltpu.VMEM((N_ACC, T, T), jnp.float32),
                    pltpu.SemaphoreType.DMA((14,)),
                ],
            ),
            out_shape=jax.ShapeDtypeStruct((ROWS, T), out_dtype),
            compiler_params=pltpu.CompilerParams(
                dimension_semantics=("arbitrary",), vmem_limit_bytes=18 * 2**20
            ),
            cost_estimate=pl.CostEstimate(
                flops=2 * 2 * SLOTS * T**3, bytes_accessed=16 * 2**20, transcendentals=0
            ),
            name="prop",
        )(meta, *pieces, own, rec, swp, inv, base)

    return call


def per_device(features, tile_values, tile_source, tile_target, tile_count, weights, bias_vector):
    blk, ch = lax.axis_index("blk"), lax.axis_index("ch")
    z, xh, y = blk // (NX * NY), (blk // NY) % NX, blk % NY
    xl, core = ch // 2, ch % 2

    swap_f = line_swap(features, 0, 0, 1)
    near = line_swap(features, 0, 1, 0)
    cross = line_swap(features, 1, 1, 0)
    over = line_swap(features, 1, 0, 0)
    swap_rest = line_swap(jnp.concatenate([near, cross, over], axis=0), 0, 0, 1)

    place = jnp.stack(
        [ch, xh, xl * 2 + core, (1 - xl) * 2 + core, xl * 2 + 1 - core, (1 - xl) * 2 + 1 - core]
    ).astype(jnp.int32)
    usable = jnp.arange(SLOTS, dtype=jnp.int32) < tile_count[0]
    squares = jnp.einsum("tij,tij->ti", tile_values, tile_values, preferred_element_type=jnp.float32)
    squares = jnp.where(usable[:, None], squares, 0.0)
    onehot = (
        (tile_target[:, None] == jnp.arange(RT, dtype=jnp.int32)[None, :]) & usable[:, None]
    ).astype(jnp.float32)
    row_norm = jnp.dot(onehot.T, squares, precision=lax.Precision.HIGHEST)
    inverse = lax.rsqrt(1.0 + row_norm)

    u0, u1, u2 = mix(
        place, [features, near, cross, over, swap_f, swap_rest], after(weights, inverse), bias_vector[None, :]
    )
    rows_1 = gather_zy(u2)
    event = rows_1[9]

    sent = lax.dynamic_slice_in_dim(tile_values, core * (SLOTS // 2), SLOTS // 2, 0)
    received = line_swap(sent, 1, 1, 0)
    swapped = line_swap(after(received, event), 0, 0, 1)

    source = jnp.where(usable, tile_source, 0)
    offset = source_rows(source, z, y)
    source_hi = (source // (RT * NY)) % NX
    slot = jnp.where(usable, (xh * 2 + source_hi) * RT + tile_target, DUMMY)
    notes = jnp.concatenate([jnp.stack([offset, slot]).astype(jnp.float32), inverse], axis=0)
    far_notes = line_swap(notes, 1, 1, 0)
    far_meta = far_notes[:2].astype(jnp.int32)
    far_meta = jnp.where(core == 0, far_meta, jnp.roll(far_meta, SLOTS // 2, axis=1))
    meta = jnp.concatenate([jnp.stack([offset, slot]).astype(jnp.int32), far_meta], axis=1).reshape(-1)
    lanes_hi = jnp.arange(T, dtype=jnp.int32)[None, :] // HALF
    inv_pair = jnp.where(
        lanes_hi == xh, inverse.reshape(-1)[:, None], far_notes[2:].reshape(-1)[:, None]
    )

    v = make_prop(2.0, jnp.bfloat16)(meta, rows_1, tile_values, received, swapped, inv_pair, u1)
    rows_2 = gather_zy(v)
    w = make_prop(1.0, jnp.bfloat16)(meta, rows_2, tile_values, received, swapped, inv_pair, u0)
    back = line_swap(w, 1, 0, 0)
    back = jnp.concatenate([back[:, HALF:], back[:, :HALF]], axis=1)
    return jnp.where(lanes_hi == xh, w, back)


def solution(mesh):
    return jax.shard_map(
        per_device,
        mesh=mesh,
        in_specs=(P("blk", "ch"), P("blk", None, None), P("blk"), P("blk"), P("blk"), P(), P()),
        out_specs=P("blk", "ch"),
        check_vma=False,
    )
```

```python
import jax
import jax.numpy as jnp
from jax import lax
from jax.experimental import pallas as pl
from jax.experimental.pallas import tpu as pltpu
from jax.sharding import PartitionSpec as P

NZ, NX, NY = 8, 2, 4
T = 128
RT = 6
ROWS = RT * T
HALF = 64
SLOTS = 128
RA = ROWS // 2
N_ACC = 4 * RT + 1
DUMMY = 4 * RT


def blk_id(z, x, y):
    return ((z % NZ) * NX + x % NX) * NY + y % NY


def shift(v, dz, dy):
    pairs = [
        (blk_id(z, x, y), blk_id(z + dz, x, y + dy))
        for z in range(NZ)
        for x in range(NX)
        for y in range(NY)
    ]
    return lax.ppermute(v, "blk", pairs)


def line_swap(v, flip_hi, flip_lo, flip_core):
    pairs = []
    for z in range(NZ):
        for xh in range(2):
            for y in range(NY):
                for xl in range(2):
                    for core in range(2):
                        src = blk_id(z, xh, y) * 4 + xl * 2 + core
                        dst = blk_id(z, xh ^ flip_hi, y) * 4 + (xl ^ flip_lo) * 2 + (core ^ flip_core)
                        pairs.append((src, dst))
    return lax.ppermute(v, ("blk", "ch"), pairs)


def ring_y(v):
    h = v.shape[0] // 2
    up, down = shift(v, 0, 1), shift(v, 0, -1)
    return [up, down, shift(up[:h], 0, 1), shift(down[h:], 0, -1)]


def ring_z(v):
    h = v.shape[0] // 2
    ups, downs = [], []
    up = down = v
    for _ in range(3):
        up, down = shift(up, 1, 0), shift(down, -1, 0)
        ups.append(up)
        downs.append(down)
    return ups + downs + [shift(up[:h], 1, 0), shift(down[h:], -1, 0)]


def gather_zy(v):
    first, second = v[:RA], v[RA:]
    near_y = ring_y(first)
    a4 = jnp.concatenate([first] + near_y, axis=0)
    b8 = jnp.concatenate([second] + ring_z(second), axis=0)
    return [a4] + ring_z(a4) + [b8] + ring_y(b8)


def after(v, event):
    return lax.optimization_barrier((v, event))[0]


def source_rows(tile, z, y):
    block, part = tile // RT, tile % RT
    dz = (block // (NX * NY) - z) % NZ
    dy = (block % NY - y) % NY
    j = jnp.where(dz == 0, 0, jnp.where(dz == 4, 7, jnp.where(dz > 4, 8 - dz, dz + 3)))
    q = jnp.where(dy == 0, 0, jnp.where(dy == 3, 1, jnp.where(dy == 1, 2, 3)))
    in_a = (j * NY + q) * RA + part * T
    in_b = NZ * NY * RA + (q * NZ + j) * RA + (part - RT // 2) * T
    return jnp.where(part < RT // 2, in_a, in_b)


def mix_kernel(place, f0, f1, f2, f3, g0, g1, w_ref, b_ref, u0_ref, u1_ref, u2_ref, w_cat):
    ch, xh = place[0], place[1]
    cols = pl.ds(pl.multiple_of(ch * T, T), T)
    for k in range(4):
        part = pl.ds(pl.multiple_of(place[2 + k] * T, T), T)
        for m in range(3):
            w_cat[k * T : (k + 1) * T, m * T : (m + 1) * T] = w_ref[m, part, cols]
    mine = lax.broadcasted_iota(jnp.int32, (T, T), 1) // HALF == xh
    bias = jnp.broadcast_to(b_ref[:, cols], (T, T))
    bias = jnp.where(mine, bias, pltpu.roll(bias, HALF, 1))
    for r in range(RT):
        rows = slice(r * T, (r + 1) * T)
        rest = [slice(k * ROWS + r * T, k * ROWS + (r + 1) * T) for k in range(3)]
        own = jnp.concatenate([f0[rows], f1[rows], g0[rows], g1[rest[0]]], axis=1)
        other = jnp.concatenate([f3[rows], f2[rows], g1[rest[2]], g1[rest[1]]], axis=1)
        u_own = jnp.dot(own, w_cat[...], preferred_element_type=jnp.float32)
        u_other = jnp.dot(other, w_cat[...], preferred_element_type=jnp.float32)
        u = [
            jnp.where(
                mine,
                u_own[:, m * T : (m + 1) * T],
                pltpu.roll(u_other[:, m * T : (m + 1) * T], HALF, 1),
            )
            for m in range(3)
        ]
        u0_ref[rows] = u[0] - u[2] + bias
        u1_ref[rows] = u[1]
        u2_ref[rows] = u[2].astype(jnp.bfloat16)


def mix(place, pieces, weights, bias):
    vmem = pl.BlockSpec(memory_space=pltpu.VMEM)
    return pl.pallas_call(
        mix_kernel,
        in_specs=[pl.BlockSpec(memory_space=pltpu.SMEM)] + [vmem] * 8,
        out_specs=[vmem] * 3,
        out_shape=[
            jax.ShapeDtypeStruct((ROWS, T), jnp.float32),
            jax.ShapeDtypeStruct((ROWS, T), jnp.float32),
            jax.ShapeDtypeStruct((ROWS, T), jnp.bfloat16),
        ],
        scratch_shapes=[pltpu.VMEM((4 * T, 3 * T), jnp.bfloat16)],
        compiler_params=pltpu.CompilerParams(vmem_limit_bytes=16 * 2**20),
        cost_estimate=pl.CostEstimate(
            flops=2 * ROWS * 1024 * 384, bytes_accessed=4 * 2**20, transcendentals=0
        ),
        name="mix",
    )(place, *pieces, weights, bias)


def add_tiles(ref, count, start, meta, x_all, acc, norms=None):
    for k in range(count):
        at = start + k
        tile = ref[k]
        off = pl.multiple_of(meta[at], T)
        acc[meta[2 * SLOTS + at]] += jnp.dot(
            tile, x_all[pl.ds(off, T), :], preferred_element_type=jnp.float32
        )
        if norms is not None:
            wide = tile.astype(jnp.float32)
            norms[meta[4 * SLOTS + at]] += wide * wide


def copy_pieces(pieces, x_all, sems):
    copies, at = [], 0
    for k, piece in enumerate(pieces):
        n = piece.shape[0]
        copies.append(pltpu.make_async_copy(piece, x_all.at[pl.ds(at, n)], sems.at[k]))
        at += n
    for c in copies:
        c.start()
    return copies


def pair_sum(acc, r):
    low = lax.broadcasted_iota(jnp.int32, (T, T), 1) < HALF
    straight = jnp.where(low, acc[r], acc[3 * RT + r])
    crossed = jnp.where(low, acc[2 * RT + r], acc[RT + r])
    return straight + pltpu.roll(crossed, HALF, 1)


def first_kernel(meta, *refs):
    pieces = refs[:14]
    own, rec, x_all, acc, norms, sems = refs[14:]
    copies = copy_pieces(pieces, x_all, sems)
    acc[...] = jnp.zeros_like(acc)
    norms[...] = jnp.zeros_like(norms)
    for c in copies:
        c.wait()

    @pl.loop(0, 4)
    def _(i):
        add_tiles(own.at[pl.ds(i * 32, 32)], 32, i * 32, meta, x_all, acc, norms)
        add_tiles(rec.at[pl.ds(i * 16, 16)], 16, SLOTS + i * 16, meta, x_all, acc, norms)


def second_kernel(meta, swp, x_all, acc_in, norms_in, base, out, inv_out, acc, norms):
    acc[...] = acc_in[...]
    norms[...] = norms_in[...]

    @pl.loop(0, 2)
    def _(i):
        at = SLOTS + SLOTS // 2 + i * 32
        add_tiles(swp.at[pl.ds(i * 32, 32)], 32, at, meta, x_all, acc, norms)

    low = lax.broadcasted_iota(jnp.int32, (T, T), 1) < HALF
    for r in range(RT):
        rows = slice(r * T, (r + 1) * T)
        low_norm = jnp.sum(norms[r], axis=1, keepdims=True)
        high_norm = jnp.sum(norms[RT + r], axis=1, keepdims=True)
        inv = lax.rsqrt(1.0 + jnp.where(low, low_norm, high_norm))
        inv_out[rows] = inv
        out[rows] = (base[rows] + 2.0 * (inv * pair_sum(acc, r))).astype(jnp.bfloat16)


def prop_first(meta, pieces, own, rec, swp_of, base):
    smem = pl.BlockSpec(memory_space=pltpu.SMEM)
    vmem = pl.BlockSpec(memory_space=pltpu.VMEM)
    shapes = [
        jax.ShapeDtypeStruct((NZ * NY * ROWS, T), jnp.bfloat16),
        jax.ShapeDtypeStruct((N_ACC, T, T), jnp.float32),
        jax.ShapeDtypeStruct((2 * RT + 1, T, T), jnp.float32),
    ]
    params = pltpu.CompilerParams(vmem_limit_bytes=16 * 2**20)
    x_all, acc, norms = pl.pallas_call(
        first_kernel,
        in_specs=[smem] + [pl.BlockSpec(memory_space=pl.ANY)] * 14 + [vmem] * 2,
        out_specs=[vmem] * 3,
        out_shape=shapes,
        scratch_shapes=[pltpu.SemaphoreType.DMA((14,))],
        compiler_params=params,
        cost_estimate=pl.CostEstimate(
            flops=3 * SLOTS * T**3, bytes_accessed=16 * 2**20, transcendentals=0
        ),
        name="prop_first",
    )(meta, *pieces, own, rec)
    return pl.pallas_call(
        second_kernel,
        in_specs=[smem] + [vmem] * 5,
        out_specs=[vmem] * 2,
        out_shape=[
            jax.ShapeDtypeStruct((ROWS, T), jnp.bfloat16),
            jax.ShapeDtypeStruct((ROWS, T), jnp.float32),
        ],
        scratch_shapes=[pltpu.VMEM(v.shape, v.dtype) for v in shapes[1:]],
        compiler_params=params,
        cost_estimate=pl.CostEstimate(
            flops=SLOTS * T**3, bytes_accessed=8 * 2**20, transcendentals=0
        ),
        name="prop_second",
    )(meta, swp_of, x_all, acc, norms, base)


def last_kernel(meta, *refs):
    pieces = refs[:14]
    own, rec, swp, inv, base, out, x_all, acc, sems = refs[14:]
    step = pl.program_id(0)

    @pl.when(step == 0)
    def _():
        copies = copy_pieces(pieces, x_all, sems)
        acc[...] = jnp.zeros_like(acc)
        for c in copies:
            c.wait()

    add_tiles(own, 32, step * 32, meta, x_all, acc)
    add_tiles(rec, 16, SLOTS + step * 16, meta, x_all, acc)
    add_tiles(swp, 16, SLOTS + SLOTS // 2 + step * 16, meta, x_all, acc)

    @pl.when(step == 3)
    def _():
        for r in range(RT):
            rows = slice(r * T, (r + 1) * T)
            out[rows] = (base[rows] + inv[rows] * pair_sum(acc, r)).astype(jnp.bfloat16)


def prop_last(meta, pieces, own, rec, swp, inv, base):
    tiles = [pl.BlockSpec((n, T, T), lambda i, m: (i, 0, 0)) for n in (32, 16, 16)]
    whole = pl.BlockSpec((ROWS, T), lambda i, m: (0, 0))
    return pl.pallas_call(
        last_kernel,
        grid_spec=pltpu.PrefetchScalarGridSpec(
            num_scalar_prefetch=1,
            grid=(4,),
            in_specs=[pl.BlockSpec(memory_space=pl.ANY)] * 14 + tiles + [whole, whole],
            out_specs=whole,
            scratch_shapes=[
                pltpu.VMEM((NZ * NY * ROWS, T), jnp.bfloat16),
                pltpu.VMEM((N_ACC, T, T), jnp.float32),
                pltpu.SemaphoreType.DMA((14,)),
            ],
        ),
        out_shape=jax.ShapeDtypeStruct((ROWS, T), jnp.bfloat16),
        compiler_params=pltpu.CompilerParams(
            dimension_semantics=("arbitrary",), vmem_limit_bytes=18 * 2**20
        ),
        cost_estimate=pl.CostEstimate(
            flops=2 * 2 * SLOTS * T**3, bytes_accessed=16 * 2**20, transcendentals=0
        ),
        name="prop_last",
    )(meta, *pieces, own, rec, swp, inv, base)


def per_device(features, tile_values, tile_source, tile_target, tile_count, weights, bias_vector):
    blk, ch = lax.axis_index("blk"), lax.axis_index("ch")
    z, xh, y = blk // (NX * NY), (blk // NY) % NX, blk % NY
    xl, core = ch // 2, ch % 2

    swap_f = line_swap(features, 0, 0, 1)
    near = line_swap(features, 0, 1, 0)
    cross = line_swap(features, 1, 1, 0)
    over = line_swap(features, 1, 0, 0)
    swap_rest = line_swap(jnp.concatenate([near, cross, over], axis=0), 0, 0, 1)

    place = jnp.stack(
        [ch, xh, xl * 2 + core, (1 - xl) * 2 + core, xl * 2 + 1 - core, (1 - xl) * 2 + 1 - core]
    ).astype(jnp.int32)
    usable = jnp.arange(SLOTS, dtype=jnp.int32) < tile_count[0]
    source = jnp.where(usable, tile_source, 0)
    offset = source_rows(source, z, y)
    source_hi = (source // (RT * NY)) % NX
    slot = jnp.where(usable, (xh * 2 + source_hi) * RT + tile_target, DUMMY)
    norm_slot = jnp.where(usable, xh * RT + tile_target, 2 * RT)
    own_meta = jnp.stack([offset, slot, norm_slot]).astype(jnp.int32)
    far_meta = line_swap(own_meta, 1, 1, 0)
    far_meta = jnp.where(core == 0, far_meta, jnp.roll(far_meta, SLOTS // 2, axis=1))
    meta = jnp.concatenate([own_meta, far_meta], axis=1).reshape(-1)

    sent = lax.dynamic_slice_in_dim(tile_values, core * (SLOTS // 2), SLOTS // 2, 0)
    mask = jnp.arange(T, dtype=jnp.int32)[None, :] // HALF == xh

    bias, meta, sent, mask, place = lax.optimization_barrier((bias_vector, meta, sent, mask, place))
    received = line_swap(sent, 1, 1, 0)
    u0, u1, u2 = mix(
        place, [features, near, cross, over, swap_f, swap_rest], weights, bias[None, :]
    )

    rows_1 = gather_zy(u2)
    last_steps = (rows_1[7], rows_1[8], rows_1[12], rows_1[13])
    swapped = line_swap(after(received, last_steps), 0, 0, 1)
    v, inv_pair = prop_first(meta, rows_1, tile_values, received, swapped, u1)
    w = prop_last(meta, gather_zy(v), tile_values, received, swapped, inv_pair, u0)
    back = line_swap(w, 1, 0, 0)
    back = jnp.concatenate([back[:, HALF:], back[:, :HALF]], axis=1)
    return jnp.where(mask, w, back)


def solution(mesh):
    return jax.shard_map(
        per_device,
        mesh=mesh,
        in_specs=(P("blk", "ch"), P("blk", None, None), P("blk"), P("blk"), P("blk"), P(), P()),
        out_specs=P("blk", "ch"),
        check_vma=False,
    )
```

```python
import jax
import jax.numpy as jnp
from jax import lax
from jax.experimental import pallas as pl
from jax.experimental.pallas import tpu as pltpu
from jax.sharding import PartitionSpec as P

NZ, NX, NY = 8, 2, 4
T = 128
RT = 6
ROWS = RT * T
HALF = 64
SLOTS = 128
RA = ROWS // 2
N_ACC = 4 * RT + 1
DUMMY = 4 * RT


def blk_id(z, x, y):
    return ((z % NZ) * NX + x % NX) * NY + y % NY


def shift(v, dz, dy):
    pairs = [
        (blk_id(z, x, y), blk_id(z + dz, x, y + dy))
        for z in range(NZ)
        for x in range(NX)
        for y in range(NY)
    ]
    return lax.ppermute(v, "blk", pairs)


def line_swap(v, flip_hi, flip_lo, flip_core):
    pairs = []
    for z in range(NZ):
        for xh in range(2):
            for y in range(NY):
                for xl in range(2):
                    for core in range(2):
                        src = blk_id(z, xh, y) * 4 + xl * 2 + core
                        dst = blk_id(z, xh ^ flip_hi, y) * 4 + (xl ^ flip_lo) * 2 + (core ^ flip_core)
                        pairs.append((src, dst))
    return lax.ppermute(v, ("blk", "ch"), pairs)


def ring_y(v):
    h = v.shape[0] // 2
    up, down = shift(v, 0, 1), shift(v, 0, -1)
    return [up, down, shift(up[:h], 0, 1), shift(down[h:], 0, -1)]


def ring_z(v):
    h = v.shape[0] // 2
    ups, downs = [], []
    up = down = v
    for _ in range(3):
        up, down = shift(up, 1, 0), shift(down, -1, 0)
        ups.append(up)
        downs.append(down)
    return ups + downs + [shift(up[:h], 1, 0), shift(down[h:], -1, 0)]


def after(v, event):
    return lax.optimization_barrier((v, event))[0]


def gather_zy(v):
    first, second = v[:RA], v[RA:]
    a4 = jnp.concatenate([first] + ring_y(first), axis=0)
    far_z = ring_z(a4)
    b8 = jnp.concatenate([second] + ring_z(second), axis=0)
    return [a4] + far_z + [b8] + ring_y(after(b8, (far_z[0], far_z[3])))


def source_rows(tile, z, y):
    block, part = tile // RT, tile % RT
    dz = (block // (NX * NY) - z) % NZ
    dy = (block % NY - y) % NY
    j = jnp.where(dz == 0, 0, jnp.where(dz == 4, 7, jnp.where(dz > 4, 8 - dz, dz + 3)))
    q = jnp.where(dy == 0, 0, jnp.where(dy == 3, 1, jnp.where(dy == 1, 2, 3)))
    in_a = (j * NY + q) * RA + part * T
    in_b = NZ * NY * RA + (q * NZ + j) * RA + (part - RT // 2) * T
    return jnp.where(part < RT // 2, in_a, in_b)


def mix_kernel(place, f0, f1, f2, f3, g0, g1, g2, g3, w_ref, b_ref, u0_ref, u1_ref, u2_ref, w_cat):
    ch, xh = place[0], place[1]
    cols = pl.ds(pl.multiple_of(ch * T, T), T)
    for k in range(4):
        part = pl.ds(pl.multiple_of(place[2 + k] * T, T), T)
        for m in range(3):
            w_cat[k * T : (k + 1) * T, m * T : (m + 1) * T] = w_ref[m, part, cols]
    mine = lax.broadcasted_iota(jnp.int32, (T, T), 1) // HALF == xh
    bias = jnp.broadcast_to(b_ref[:, cols], (T, T))
    bias = jnp.where(mine, bias, pltpu.roll(bias, HALF, 1))
    for r in range(RT):
        rows = slice(r * T, (r + 1) * T)
        own = jnp.concatenate([f0[rows], f1[rows], g0[rows], g1[rows]], axis=1)
        other = jnp.concatenate([f3[rows], f2[rows], g3[rows], g2[rows]], axis=1)
        u_own = jnp.dot(own, w_cat[...], preferred_element_type=jnp.float32)
        u_other = jnp.dot(other, w_cat[...], preferred_element_type=jnp.float32)
        u = [
            jnp.where(
                mine,
                u_own[:, m * T : (m + 1) * T],
                pltpu.roll(u_other[:, m * T : (m + 1) * T], HALF, 1),
            )
            for m in range(3)
        ]
        u0_ref[rows] = u[0] - u[2] + bias
        u1_ref[rows] = u[1]
        u2_ref[rows] = u[2].astype(jnp.bfloat16)


def mix(place, pieces, weights, bias):
    vmem = pl.BlockSpec(memory_space=pltpu.VMEM)
    return pl.pallas_call(
        mix_kernel,
        in_specs=[pl.BlockSpec(memory_space=pltpu.SMEM)] + [vmem] * 10,
        out_specs=[vmem] * 3,
        out_shape=[
            jax.ShapeDtypeStruct((ROWS, T), jnp.float32),
            jax.ShapeDtypeStruct((ROWS, T), jnp.float32),
            jax.ShapeDtypeStruct((ROWS, T), jnp.bfloat16),
        ],
        scratch_shapes=[pltpu.VMEM((4 * T, 3 * T), jnp.bfloat16)],
        compiler_params=pltpu.CompilerParams(vmem_limit_bytes=16 * 2**20),
        cost_estimate=pl.CostEstimate(
            flops=2 * ROWS * 1024 * 384, bytes_accessed=4 * 2**20, transcendentals=0
        ),
        name="mix",
    )(place, *pieces, weights, bias)


def add_tiles(ref, count, start, meta, x_all, acc, norms=None):
    for k in range(count):
        at = start + k
        tile = ref[k]
        off = pl.multiple_of(meta[at], T)
        acc[meta[2 * SLOTS + at]] += jnp.dot(
            tile, x_all[pl.ds(off, T), :], preferred_element_type=jnp.float32
        )
        if norms is not None:
            wide = tile.astype(jnp.float32)
            norms[meta[4 * SLOTS + at]] += wide * wide


def copy_pieces(pieces, x_all, sems):
    copies, at = [], 0
    for k, piece in enumerate(pieces):
        n = piece.shape[0]
        copies.append(pltpu.make_async_copy(piece, x_all.at[pl.ds(at, n)], sems.at[k]))
        at += n
    for c in copies:
        c.start()
    return copies


def pair_sum(acc, r):
    low = lax.broadcasted_iota(jnp.int32, (T, T), 1) < HALF
    straight = jnp.where(low, acc[r], acc[3 * RT + r])
    crossed = jnp.where(low, acc[2 * RT + r], acc[RT + r])
    return straight + pltpu.roll(crossed, HALF, 1)


def first_kernel(meta, *refs):
    pieces = refs[:14]
    own, rec, x_all, acc, norms, sems = refs[14:]
    copies = copy_pieces(pieces, x_all, sems)
    acc[...] = jnp.zeros_like(acc)
    norms[...] = jnp.zeros_like(norms)
    for c in copies:
        c.wait()

    @pl.loop(0, 4)
    def _(i):
        add_tiles(own.at[pl.ds(i * 32, 32)], 32, i * 32, meta, x_all, acc, norms)
        add_tiles(rec.at[pl.ds(i * 16, 16)], 16, SLOTS + i * 16, meta, x_all, acc, norms)


def second_kernel(meta, swp, x_all, acc_in, norms_in, base, out, inv_out, acc, norms):
    acc[...] = acc_in[...]
    norms[...] = norms_in[...]

    @pl.loop(0, 2)
    def _(i):
        at = SLOTS + SLOTS // 2 + i * 32
        add_tiles(swp.at[pl.ds(i * 32, 32)], 32, at, meta, x_all, acc, norms)

    low = lax.broadcasted_iota(jnp.int32, (T, T), 1) < HALF
    for r in range(RT):
        rows = slice(r * T, (r + 1) * T)
        low_norm = jnp.sum(norms[r], axis=1, keepdims=True)
        high_norm = jnp.sum(norms[RT + r], axis=1, keepdims=True)
        inv = lax.rsqrt(1.0 + jnp.where(low, low_norm, high_norm))
        inv_out[rows] = inv
        out[rows] = (base[rows] + 2.0 * (inv * pair_sum(acc, r))).astype(jnp.bfloat16)


def prop_first(meta, pieces, own, rec, swp_of, base):
    smem = pl.BlockSpec(memory_space=pltpu.SMEM)
    vmem = pl.BlockSpec(memory_space=pltpu.VMEM)
    shapes = [
        jax.ShapeDtypeStruct((NZ * NY * ROWS, T), jnp.bfloat16),
        jax.ShapeDtypeStruct((N_ACC, T, T), jnp.float32),
        jax.ShapeDtypeStruct((2 * RT + 1, T, T), jnp.float32),
    ]
    params = pltpu.CompilerParams(vmem_limit_bytes=16 * 2**20)
    x_all, acc, norms = pl.pallas_call(
        first_kernel,
        in_specs=[smem] + [pl.BlockSpec(memory_space=pl.ANY)] * 14 + [vmem] * 2,
        out_specs=[vmem] * 3,
        out_shape=shapes,
        scratch_shapes=[pltpu.SemaphoreType.DMA((14,))],
        compiler_params=params,
        cost_estimate=pl.CostEstimate(
            flops=3 * SLOTS * T**3, bytes_accessed=16 * 2**20, transcendentals=0
        ),
        name="prop_first",
    )(meta, *pieces, own, rec)
    return pl.pallas_call(
        second_kernel,
        in_specs=[smem] + [vmem] * 5,
        out_specs=[vmem] * 2,
        out_shape=[
            jax.ShapeDtypeStruct((ROWS, T), jnp.bfloat16),
            jax.ShapeDtypeStruct((ROWS, T), jnp.float32),
        ],
        scratch_shapes=[pltpu.VMEM(v.shape, v.dtype) for v in shapes[1:]],
        compiler_params=params,
        cost_estimate=pl.CostEstimate(
            flops=SLOTS * T**3, bytes_accessed=8 * 2**20, transcendentals=0
        ),
        name="prop_second",
    )(meta, swp_of, x_all, acc, norms, base)


def last_kernel(meta, *refs):
    pieces = refs[:14]
    own, rec, swp, inv, base, out, pack, x_all, acc, sems = refs[14:]
    step = pl.program_id(0)

    @pl.when(step == 0)
    def _():
        copies = copy_pieces(pieces, x_all, sems)
        acc[...] = jnp.zeros_like(acc)
        for c in copies:
            c.wait()

    add_tiles(own, 32, step * 32, meta, x_all, acc)
    add_tiles(rec, 16, SLOTS + step * 16, meta, x_all, acc)
    add_tiles(swp, 16, SLOTS + SLOTS // 2 + step * 16, meta, x_all, acc)

    @pl.when(step == 3)
    def _():
        lane_half = lax.broadcasted_iota(jnp.int32, (T, T), 1) // HALF
        low, stay = lane_half == 0, lane_half != meta[6 * SLOTS]
        for r in range(RT // 2):
            done = []
            for k in (r, r + RT // 2):
                rows = slice(k * T, (k + 1) * T)
                done.append(base[rows] + inv[rows] * pair_sum(acc, k))
                out[rows] = done[-1].astype(jnp.bfloat16)
            same = jnp.where(low, done[0], done[1])
            moved = pltpu.roll(jnp.where(low, done[1], done[0]), HALF, 1)
            pack[r * T : (r + 1) * T] = jnp.where(stay, same, moved).astype(jnp.bfloat16)


def prop_last(meta, pieces, own, rec, swp, inv, base):
    tiles = [pl.BlockSpec((n, T, T), lambda i, m: (i, 0, 0)) for n in (32, 16, 16)]
    whole = pl.BlockSpec((ROWS, T), lambda i, m: (0, 0))
    return pl.pallas_call(
        last_kernel,
        grid_spec=pltpu.PrefetchScalarGridSpec(
            num_scalar_prefetch=1,
            grid=(4,),
            in_specs=[pl.BlockSpec(memory_space=pl.ANY)] * 14 + tiles + [whole, whole],
            out_specs=[whole, pl.BlockSpec((ROWS // 2, T), lambda i, m: (0, 0))],
            scratch_shapes=[
                pltpu.VMEM((NZ * NY * ROWS, T), jnp.bfloat16),
                pltpu.VMEM((N_ACC, T, T), jnp.float32),
                pltpu.SemaphoreType.DMA((14,)),
            ],
        ),
        out_shape=[
            jax.ShapeDtypeStruct((ROWS, T), jnp.bfloat16),
            jax.ShapeDtypeStruct((ROWS // 2, T), jnp.bfloat16),
        ],
        compiler_params=pltpu.CompilerParams(
            dimension_semantics=("arbitrary",), vmem_limit_bytes=18 * 2**20
        ),
        cost_estimate=pl.CostEstimate(
            flops=2 * 2 * SLOTS * T**3, bytes_accessed=16 * 2**20, transcendentals=0
        ),
        name="prop_last",
    )(meta, *pieces, own, rec, swp, inv, base)


def per_device(features, tile_values, tile_source, tile_target, tile_count, weights, bias_vector):
    blk, ch = lax.axis_index("blk"), lax.axis_index("ch")
    z, xh, y = blk // (NX * NY), (blk // NY) % NX, blk % NY
    xl, core = ch // 2, ch % 2

    swap_f = line_swap(features, 0, 0, 1)
    near = line_swap(features, 0, 1, 0)
    cross = line_swap(features, 1, 1, 0)
    over = line_swap(features, 1, 0, 0)
    swap_rest = [line_swap(v, 0, 0, 1) for v in (near, cross, over)]

    place = jnp.stack(
        [ch, xh, xl * 2 + core, (1 - xl) * 2 + core, xl * 2 + 1 - core, (1 - xl) * 2 + 1 - core]
    ).astype(jnp.int32)
    usable = jnp.arange(SLOTS, dtype=jnp.int32) < tile_count[0]
    source = jnp.where(usable, tile_source, 0)
    offset = source_rows(source, z, y)
    source_hi = (source // (RT * NY)) % NX
    slot = jnp.where(usable, (xh * 2 + source_hi) * RT + tile_target, DUMMY)
    norm_slot = jnp.where(usable, xh * RT + tile_target, 2 * RT)
    own_meta = jnp.stack([offset, slot, norm_slot]).astype(jnp.int32)
    far_meta = line_swap(own_meta, 1, 1, 0)
    far_meta = jnp.where(core == 0, far_meta, jnp.roll(far_meta, SLOTS // 2, axis=1))
    meta = jnp.concatenate([own_meta, far_meta], axis=1).reshape(-1)
    meta = jnp.concatenate([meta, xh.astype(jnp.int32)[None]])

    sent = lax.dynamic_slice_in_dim(tile_values, core * (SLOTS // 2), SLOTS // 2, 0)
    mask = jnp.arange(T, dtype=jnp.int32)[None, :] // HALF == xh

    received = line_swap(sent, 1, 1, 0)
    bias, meta, _, mask, place = lax.optimization_barrier((bias_vector, meta, sent, mask, place))
    u0, u1, u2 = mix(
        place, [features, near, cross, over, swap_f, *swap_rest], weights, bias[None, :]
    )

    rows_1 = gather_zy(u2)
    last_steps = (rows_1[7], rows_1[8], rows_1[12], rows_1[13])
    swapped = line_swap(after(received, last_steps), 0, 0, 1)
    v, inv_pair = prop_first(meta, rows_1, tile_values, received, swapped, u1)
    w, pack = prop_last(meta, gather_zy(v), tile_values, received, swapped, inv_pair, u0)
    back = line_swap(pack, 1, 0, 0)
    back = jnp.concatenate([back[:, :HALF], back[:, HALF:]], axis=0)
    back = jnp.concatenate([back, back], axis=1)
    return jnp.where(mask, w, back)


def solution(mesh):
    return jax.shard_map(
        per_device,
        mesh=mesh,
        in_specs=(P("blk", "ch"), P("blk", None, None), P("blk"), P("blk"), P("blk"), P(), P()),
        out_specs=P("blk", "ch"),
        check_vma=False,
    )
```

```python
import jax
import jax.numpy as jnp
from jax import lax
from jax.experimental import pallas as pl
from jax.experimental.pallas import tpu as pltpu
from jax.sharding import PartitionSpec as P

NZ, NX, NY = 8, 2, 4
T = 128
RT = 6
ROWS = RT * T
HALF = 64
SLOTS = 128
RA = ROWS // 2
N_ACC = 4 * RT + 1
DUMMY = 4 * RT


def blk_id(z, x, y):
    return ((z % NZ) * NX + x % NX) * NY + y % NY


def shift(v, dz, dy):
    pairs = [
        (blk_id(z, x, y), blk_id(z + dz, x, y + dy))
        for z in range(NZ)
        for x in range(NX)
        for y in range(NY)
    ]
    return lax.ppermute(v, "blk", pairs)


def line_swap(v, flip_hi, flip_lo, flip_core):
    pairs = []
    for z in range(NZ):
        for xh in range(2):
            for y in range(NY):
                for xl in range(2):
                    for core in range(2):
                        src = blk_id(z, xh, y) * 4 + xl * 2 + core
                        dst = blk_id(z, xh ^ flip_hi, y) * 4 + (xl ^ flip_lo) * 2 + (core ^ flip_core)
                        pairs.append((src, dst))
    return lax.ppermute(v, ("blk", "ch"), pairs)


def ring_y(v):
    h = v.shape[0] // 2
    up, down = shift(v, 0, 1), shift(v, 0, -1)
    return [up, down, shift(up[:h], 0, 1), shift(down[h:], 0, -1)]


def ring_z(v):
    h = v.shape[0] // 2
    ups, downs = [], []
    up = down = v
    for _ in range(3):
        up, down = shift(up, 1, 0), shift(down, -1, 0)
        ups.append(up)
        downs.append(down)
    return ups + downs + [shift(up[:h], 1, 0), shift(down[h:], -1, 0)]


def after(v, event):
    return lax.optimization_barrier((v, event))[0]


def gather_zy(v):
    first, second = v[:RA], v[RA:]
    a4 = jnp.concatenate([first] + ring_y(first), axis=0)
    far_z = ring_z(a4)
    b8 = jnp.concatenate([second] + ring_z(second), axis=0)
    return [a4] + far_z + [b8] + ring_y(after(b8, (far_z[0], far_z[3])))


def source_rows(tile, z, y):
    block, part = tile // RT, tile % RT
    dz = (block // (NX * NY) - z) % NZ
    dy = (block % NY - y) % NY
    j = jnp.where(dz == 0, 0, jnp.where(dz == 4, 7, jnp.where(dz > 4, 8 - dz, dz + 3)))
    q = jnp.where(dy == 0, 0, jnp.where(dy == 3, 1, jnp.where(dy == 1, 2, 3)))
    in_a = (j * NY + q) * RA + part * T
    in_b = NZ * NY * RA + (q * NZ + j) * RA + (part - RT // 2) * T
    return jnp.where(part < RT // 2, in_a, in_b)


def mix_kernel(place, f0, f1, f2, f3, g0, g1, g2, g3, w_ref, b_ref, u0_ref, u1_ref, u2_ref, w_cat):
    ch, xh = place[0], place[1]
    cols = pl.ds(pl.multiple_of(ch * T, T), T)
    for k in range(4):
        part = pl.ds(pl.multiple_of(place[2 + k] * T, T), T)
        for m in range(3):
            w_cat[k * T : (k + 1) * T, m * T : (m + 1) * T] = w_ref[m, part, cols]
    mine = lax.broadcasted_iota(jnp.int32, (T, T), 1) // HALF == xh
    bias = jnp.broadcast_to(b_ref[:, cols], (T, T))
    bias = jnp.where(mine, bias, pltpu.roll(bias, HALF, 1))
    for r in range(RT):
        rows = slice(r * T, (r + 1) * T)
        own = jnp.concatenate([f0[rows], f1[rows], g0[rows], g1[rows]], axis=1)
        other = jnp.concatenate([f3[rows], f2[rows], g3[rows], g2[rows]], axis=1)
        u_own = jnp.dot(own, w_cat[...], preferred_element_type=jnp.float32)
        u_other = jnp.dot(other, w_cat[...], preferred_element_type=jnp.float32)
        u = [
            jnp.where(
                mine,
                u_own[:, m * T : (m + 1) * T],
                pltpu.roll(u_other[:, m * T : (m + 1) * T], HALF, 1),
            )
            for m in range(3)
        ]
        u0_ref[rows] = u[0] - u[2] + bias
        u1_ref[rows] = u[1]
        u2_ref[rows] = u[2].astype(jnp.bfloat16)


def mix(place, pieces, weights, bias):
    vmem = pl.BlockSpec(memory_space=pltpu.VMEM)
    return pl.pallas_call(
        mix_kernel,
        in_specs=[pl.BlockSpec(memory_space=pltpu.SMEM)] + [vmem] * 10,
        out_specs=[vmem] * 3,
        out_shape=[
            jax.ShapeDtypeStruct((ROWS, T), jnp.float32),
            jax.ShapeDtypeStruct((ROWS, T), jnp.float32),
            jax.ShapeDtypeStruct((ROWS, T), jnp.bfloat16),
        ],
        scratch_shapes=[pltpu.VMEM((4 * T, 3 * T), jnp.bfloat16)],
        compiler_params=pltpu.CompilerParams(vmem_limit_bytes=16 * 2**20),
        cost_estimate=pl.CostEstimate(
            flops=2 * ROWS * 1024 * 384, bytes_accessed=4 * 2**20, transcendentals=0
        ),
        name="mix",
    )(place, *pieces, weights, bias)


def add_tiles(ref, count, start, meta, x_all, acc, norms=None):
    for k in range(count):
        at = start + k
        tile = ref[k]
        off = pl.multiple_of(meta[at], T)
        acc[meta[2 * SLOTS + at]] += jnp.dot(
            tile, x_all[pl.ds(off, T), :], preferred_element_type=jnp.float32
        )
        if norms is not None:
            wide = tile.astype(jnp.float32)
            norms[meta[4 * SLOTS + at]] += wide * wide


def copy_pieces(pieces, x_all):
    at = 0
    for piece in pieces:
        n = piece.shape[0]

        @pl.loop(0, n // 256)
        def _(i, piece=piece, at=at):
            low = pl.multiple_of(i * 256, 256)
            x_all[pl.ds(at + low, 256), :] = piece[pl.ds(low, 256), :]

        at += n


def pair_sum(acc, r):
    low = lax.broadcasted_iota(jnp.int32, (T, T), 1) < HALF
    straight = jnp.where(low, acc[r], acc[3 * RT + r])
    crossed = jnp.where(low, acc[2 * RT + r], acc[RT + r])
    return straight + pltpu.roll(crossed, HALF, 1)


def first_kernel(meta, *refs):
    pieces = refs[:14]
    own, rec, x_all, acc, norms = refs[14:]
    copy_pieces(pieces, x_all)
    acc[...] = jnp.zeros_like(acc)
    norms[...] = jnp.zeros_like(norms)

    @pl.loop(0, 4)
    def _(i):
        add_tiles(own.at[pl.ds(i * 32, 32)], 32, i * 32, meta, x_all, acc, norms)
        add_tiles(rec.at[pl.ds(i * 16, 16)], 16, SLOTS + i * 16, meta, x_all, acc, norms)


def second_kernel(meta, swp, x_all, acc_in, norms_in, base, out, inv_out, acc, norms):
    acc[...] = acc_in[...]
    norms[...] = norms_in[...]

    @pl.loop(0, 2)
    def _(i):
        at = SLOTS + SLOTS // 2 + i * 32
        add_tiles(swp.at[pl.ds(i * 32, 32)], 32, at, meta, x_all, acc, norms)

    low = lax.broadcasted_iota(jnp.int32, (T, T), 1) < HALF
    for r in range(RT):
        rows = slice(r * T, (r + 1) * T)
        low_norm = jnp.sum(norms[r], axis=1, keepdims=True)
        high_norm = jnp.sum(norms[RT + r], axis=1, keepdims=True)
        inv = lax.rsqrt(1.0 + jnp.where(low, low_norm, high_norm))
        inv_out[rows] = inv
        out[rows] = (base[rows] + 2.0 * (inv * pair_sum(acc, r))).astype(jnp.bfloat16)


def prop_first(meta, pieces, own, rec, swp_of, base):
    smem = pl.BlockSpec(memory_space=pltpu.SMEM)
    vmem = pl.BlockSpec(memory_space=pltpu.VMEM)
    shapes = [
        jax.ShapeDtypeStruct((NZ * NY * ROWS, T), jnp.bfloat16),
        jax.ShapeDtypeStruct((N_ACC, T, T), jnp.float32),
        jax.ShapeDtypeStruct((2 * RT + 1, T, T), jnp.float32),
    ]
    params = pltpu.CompilerParams(vmem_limit_bytes=16 * 2**20)
    x_all, acc, norms = pl.pallas_call(
        first_kernel,
        in_specs=[smem] + [vmem] * 16,
        out_specs=[vmem] * 3,
        out_shape=shapes,
        compiler_params=params,
        cost_estimate=pl.CostEstimate(
            flops=3 * SLOTS * T**3, bytes_accessed=16 * 2**20, transcendentals=0
        ),
        name="prop_first",
    )(meta, *pieces, own, rec)
    return pl.pallas_call(
        second_kernel,
        in_specs=[smem] + [vmem] * 5,
        out_specs=[vmem] * 2,
        out_shape=[
            jax.ShapeDtypeStruct((ROWS, T), jnp.bfloat16),
            jax.ShapeDtypeStruct((ROWS, T), jnp.float32),
        ],
        scratch_shapes=[pltpu.VMEM(v.shape, v.dtype) for v in shapes[1:]],
        compiler_params=params,
        cost_estimate=pl.CostEstimate(
            flops=SLOTS * T**3, bytes_accessed=8 * 2**20, transcendentals=0
        ),
        name="prop_second",
    )(meta, swp_of, x_all, acc, norms, base)


def last_kernel(meta, *refs):
    pieces = refs[:14]
    own, rec, swp, inv, base, out, pack, x_all, acc = refs[14:]
    copy_pieces(pieces, x_all)
    acc[...] = jnp.zeros_like(acc)

    @pl.loop(0, 4)
    def _(i):
        add_tiles(own.at[pl.ds(i * 32, 32)], 32, i * 32, meta, x_all, acc)
        add_tiles(rec.at[pl.ds(i * 16, 16)], 16, SLOTS + i * 16, meta, x_all, acc)
        add_tiles(swp.at[pl.ds(i * 16, 16)], 16, SLOTS + SLOTS // 2 + i * 16, meta, x_all, acc)

    lane_half = lax.broadcasted_iota(jnp.int32, (T, T), 1) // HALF
    low, stay = lane_half == 0, lane_half != meta[6 * SLOTS]
    for r in range(RT // 2):
        done = []
        for k in (r, r + RT // 2):
            rows = slice(k * T, (k + 1) * T)
            done.append(base[rows] + inv[rows] * pair_sum(acc, k))
            out[rows] = done[-1].astype(jnp.bfloat16)
        same = jnp.where(low, done[0], done[1])
        moved = pltpu.roll(jnp.where(low, done[1], done[0]), HALF, 1)
        pack[r * T : (r + 1) * T] = jnp.where(stay, same, moved).astype(jnp.bfloat16)


def prop_last(meta, pieces, own, rec, swp, inv, base):
    vmem = pl.BlockSpec(memory_space=pltpu.VMEM)
    return pl.pallas_call(
        last_kernel,
        in_specs=[pl.BlockSpec(memory_space=pltpu.SMEM)] + [vmem] * 19,
        out_specs=[vmem] * 2,
        out_shape=[
            jax.ShapeDtypeStruct((ROWS, T), jnp.bfloat16),
            jax.ShapeDtypeStruct((ROWS // 2, T), jnp.bfloat16),
        ],
        scratch_shapes=[
            pltpu.VMEM((NZ * NY * ROWS, T), jnp.bfloat16),
            pltpu.VMEM((N_ACC, T, T), jnp.float32),
        ],
        compiler_params=pltpu.CompilerParams(vmem_limit_bytes=16 * 2**20),
        cost_estimate=pl.CostEstimate(
            flops=2 * 2 * SLOTS * T**3, bytes_accessed=16 * 2**20, transcendentals=0
        ),
        name="prop_last",
    )(meta, *pieces, own, rec, swp, inv, base)


def per_device(features, tile_values, tile_source, tile_target, tile_count, weights, bias_vector):
    blk, ch = lax.axis_index("blk"), lax.axis_index("ch")
    z, xh, y = blk // (NX * NY), (blk // NY) % NX, blk % NY
    xl, core = ch // 2, ch % 2

    swap_f = line_swap(features, 0, 0, 1)
    near = line_swap(features, 0, 1, 0)
    cross = line_swap(features, 1, 1, 0)
    over = line_swap(features, 1, 0, 0)
    swap_rest = [line_swap(v, 0, 0, 1) for v in (near, cross, over)]

    place = jnp.stack(
        [ch, xh, xl * 2 + core, (1 - xl) * 2 + core, xl * 2 + 1 - core, (1 - xl) * 2 + 1 - core]
    ).astype(jnp.int32)
    usable = jnp.arange(SLOTS, dtype=jnp.int32) < tile_count[0]
    source = jnp.where(usable, tile_source, 0)
    offset = source_rows(source, z, y)
    source_hi = (source // (RT * NY)) % NX
    slot = jnp.where(usable, (xh * 2 + source_hi) * RT + tile_target, DUMMY)
    norm_slot = jnp.where(usable, xh * RT + tile_target, 2 * RT)
    own_meta = jnp.stack([offset, slot, norm_slot]).astype(jnp.int32)
    far_meta = line_swap(own_meta, 1, 1, 0)
    far_meta = jnp.where(core == 0, far_meta, jnp.roll(far_meta, SLOTS // 2, axis=1))
    meta = jnp.concatenate([own_meta, far_meta], axis=1).reshape(-1)
    meta = jnp.concatenate([meta, xh.astype(jnp.int32)[None]])

    sent = lax.dynamic_slice_in_dim(tile_values, core * (SLOTS // 2), SLOTS // 2, 0)
    mask = jnp.arange(T, dtype=jnp.int32)[None, :] // HALF == xh

    received = line_swap(sent, 1, 1, 0)
    bias, meta, _, mask, place = lax.optimization_barrier((bias_vector, meta, sent, mask, place))
    u0, u1, u2 = mix(
        place, [features, near, cross, over, swap_f, *swap_rest], weights, bias[None, :]
    )

    rows_1 = gather_zy(u2)
    last_steps = (rows_1[7], rows_1[8], rows_1[12], rows_1[13])
    swapped = line_swap(after(received, last_steps), 0, 0, 1)
    v, inv_pair = prop_first(meta, rows_1, tile_values, received, swapped, u1)
    w, pack = prop_last(meta, gather_zy(v), tile_values, received, swapped, inv_pair, u0)
    back = line_swap(pack, 1, 0, 0)
    back = jnp.concatenate([back[:, :HALF], back[:, HALF:]], axis=0)
    back = jnp.concatenate([back, back], axis=1)
    return jnp.where(mask, w, back)


def solution(mesh):
    return jax.shard_map(
        per_device,
        mesh=mesh,
        in_specs=(P("blk", "ch"), P("blk", None, None), P("blk"), P("blk"), P("blk"), P(), P()),
        out_specs=P("blk", "ch"),
        check_vma=False,
    )
```

```python
import jax
import jax.numpy as jnp
from jax import lax
from jax.experimental import pallas as pl
from jax.experimental.pallas import tpu as pltpu
from jax.sharding import PartitionSpec as P

NZ, NX, NY = 8, 2, 4
T = 128
RT = 6
ROWS = RT * T
HALF = 64
SLOTS = 128
RA = ROWS // 2
N_ACC = 4 * RT + 1
DUMMY = 4 * RT


def blk_id(z, x, y):
    return ((z % NZ) * NX + x % NX) * NY + y % NY


def shift(v, dz, dy):
    pairs = [
        (blk_id(z, x, y), blk_id(z + dz, x, y + dy))
        for z in range(NZ)
        for x in range(NX)
        for y in range(NY)
    ]
    return lax.ppermute(v, "blk", pairs)


def line_swap(v, flip_hi, flip_lo, flip_core):
    pairs = []
    for z in range(NZ):
        for xh in range(2):
            for y in range(NY):
                for xl in range(2):
                    for core in range(2):
                        src = blk_id(z, xh, y) * 4 + xl * 2 + core
                        dst = blk_id(z, xh ^ flip_hi, y) * 4 + (xl ^ flip_lo) * 2 + (core ^ flip_core)
                        pairs.append((src, dst))
    return lax.ppermute(v, ("blk", "ch"), pairs)


def ring_y(v):
    h = v.shape[0] // 2
    up, down = shift(v, 0, 1), shift(v, 0, -1)
    return [up, down, shift(up[:h], 0, 1), shift(down[h:], 0, -1)]


def ring_z(v):
    h = v.shape[0] // 2
    ups, downs = [], []
    up = down = v
    for _ in range(3):
        up, down = shift(up, 1, 0), shift(down, -1, 0)
        ups.append(up)
        downs.append(down)
    return ups + downs + [shift(up[:h], 1, 0), shift(down[h:], -1, 0)]


def after(v, event):
    return lax.optimization_barrier((v, event))[0]


def gather_zy(v):
    first, second = v[:RA], v[RA:]
    a4 = jnp.concatenate([first] + ring_y(first), axis=0)
    far_z = ring_z(a4)
    b8 = jnp.concatenate([second] + ring_z(second), axis=0)
    return [a4] + far_z + [b8] + ring_y(after(b8, (far_z[0], far_z[3])))


def source_rows(tile, z, y):
    block, part = tile // RT, tile % RT
    dz = (block // (NX * NY) - z) % NZ
    dy = (block % NY - y) % NY
    j = jnp.where(dz == 0, 0, jnp.where(dz == 4, 7, jnp.where(dz > 4, 8 - dz, dz + 3)))
    q = jnp.where(dy == 0, 0, jnp.where(dy == 3, 1, jnp.where(dy == 1, 2, 3)))
    in_a = (j * NY + q) * RA + part * T
    in_b = NZ * NY * RA + (q * NZ + j) * RA + (part - RT // 2) * T
    return jnp.where(part < RT // 2, in_a, in_b)


def mix_kernel(place, f0, f1, f2, f3, g0, g1, g2, g3, w_ref, b_ref, u0_ref, u1_ref, u2_ref, w_cat):
    ch, xh = place[0], place[1]
    cols = pl.ds(pl.multiple_of(ch * T, T), T)
    for k in range(4):
        part = pl.ds(pl.multiple_of(place[2 + k] * T, T), T)
        for m in range(3):
            w_cat[k * T : (k + 1) * T, m * T : (m + 1) * T] = w_ref[m, part, cols]
    mine = lax.broadcasted_iota(jnp.int32, (T, T), 1) // HALF == xh
    bias = jnp.broadcast_to(b_ref[:, cols], (T, T))
    bias = jnp.where(mine, bias, pltpu.roll(bias, HALF, 1))
    for r in range(RT):
        rows = slice(r * T, (r + 1) * T)
        own = jnp.concatenate([f0[rows], f1[rows], g0[rows], g1[rows]], axis=1)
        other = jnp.concatenate([f3[rows], f2[rows], g3[rows], g2[rows]], axis=1)
        u_own = jnp.dot(own, w_cat[...], preferred_element_type=jnp.float32)
        u_other = jnp.dot(other, w_cat[...], preferred_element_type=jnp.float32)
        u = [
            jnp.where(
                mine,
                u_own[:, m * T : (m + 1) * T],
                pltpu.roll(u_other[:, m * T : (m + 1) * T], HALF, 1),
            )
            for m in range(3)
        ]
        u0_ref[rows] = u[0] - u[2] + bias
        u1_ref[rows] = u[1]
        u2_ref[rows] = u[2].astype(jnp.bfloat16)


def mix(place, pieces, weights, bias):
    vmem = pl.BlockSpec(memory_space=pltpu.VMEM)
    return pl.pallas_call(
        mix_kernel,
        in_specs=[pl.BlockSpec(memory_space=pltpu.SMEM)] + [vmem] * 10,
        out_specs=[vmem] * 3,
        out_shape=[
            jax.ShapeDtypeStruct((ROWS, T), jnp.float32),
            jax.ShapeDtypeStruct((ROWS, T), jnp.float32),
            jax.ShapeDtypeStruct((ROWS, T), jnp.bfloat16),
        ],
        scratch_shapes=[pltpu.VMEM((4 * T, 3 * T), jnp.bfloat16)],
        compiler_params=pltpu.CompilerParams(vmem_limit_bytes=16 * 2**20),
        cost_estimate=pl.CostEstimate(
            flops=2 * ROWS * 1024 * 384, bytes_accessed=4 * 2**20, transcendentals=0
        ),
        name="mix",
    )(place, *pieces, weights, bias)


def add_tiles(ref, count, start, meta, x_all, acc, norms=None):
    for k in range(count):
        at = start + k
        tile = ref[k]
        off = pl.multiple_of(meta[at], T)
        acc[meta[2 * SLOTS + at]] += jnp.dot(
            tile, x_all[pl.ds(off, T), :], preferred_element_type=jnp.float32
        )
        if norms is not None:
            wide = tile.astype(jnp.float32)
            norms[meta[4 * SLOTS + at]] += wide * wide


def copy_pieces(pieces, x_all):
    at = 0
    for piece in pieces:
        n = piece.shape[0]

        @pl.loop(0, n // 256)
        def _(i, piece=piece, at=at):
            low = pl.multiple_of(i * 256, 256)
            x_all[pl.ds(at + low, 256), :] = piece[pl.ds(low, 256), :]

        at += n


def pair_sum(acc, r):
    low = lax.broadcasted_iota(jnp.int32, (T, T), 1) < HALF
    straight = jnp.where(low, acc[r], acc[3 * RT + r])
    crossed = jnp.where(low, acc[2 * RT + r], acc[RT + r])
    return straight + pltpu.roll(crossed, HALF, 1)


def first_kernel(meta, *refs):
    pieces = refs[:14]
    own, rec, x_all, acc, norms = refs[14:]
    copy_pieces(pieces, x_all)
    acc[...] = jnp.zeros_like(acc)
    norms[...] = jnp.zeros_like(norms)

    @pl.loop(0, 2)
    def _(i):
        add_tiles(own.at[pl.ds(i * 64, 64)], 64, i * 64, meta, x_all, acc, norms)
        add_tiles(rec.at[pl.ds(i * 32, 32)], 32, SLOTS + i * 32, meta, x_all, acc, norms)


def second_kernel(meta, swp, x_all, acc_in, norms_in, base, out, inv_out, acc, norms):
    acc[...] = acc_in[...]
    norms[...] = norms_in[...]

    @pl.loop(0, 2)
    def _(i):
        at = SLOTS + SLOTS // 2 + i * 32
        add_tiles(swp.at[pl.ds(i * 32, 32)], 32, at, meta, x_all, acc, norms)

    low = lax.broadcasted_iota(jnp.int32, (T, T), 1) < HALF
    for r in range(RT):
        rows = slice(r * T, (r + 1) * T)
        low_norm = jnp.sum(norms[r], axis=1, keepdims=True)
        high_norm = jnp.sum(norms[RT + r], axis=1, keepdims=True)
        inv = lax.rsqrt(1.0 + jnp.where(low, low_norm, high_norm))
        inv_out[rows] = inv
        out[rows] = (base[rows] + 2.0 * (inv * pair_sum(acc, r))).astype(jnp.bfloat16)


def prop_first(meta, pieces, own, rec, swp_of, base):
    smem = pl.BlockSpec(memory_space=pltpu.SMEM)
    vmem = pl.BlockSpec(memory_space=pltpu.VMEM)
    shapes = [
        jax.ShapeDtypeStruct((NZ * NY * ROWS, T), jnp.bfloat16),
        jax.ShapeDtypeStruct((N_ACC, T, T), jnp.float32),
        jax.ShapeDtypeStruct((2 * RT + 1, T, T), jnp.float32),
    ]
    params = pltpu.CompilerParams(vmem_limit_bytes=16 * 2**20)
    x_all, acc, norms = pl.pallas_call(
        first_kernel,
        in_specs=[smem] + [vmem] * 16,
        out_specs=[vmem] * 3,
        out_shape=shapes,
        compiler_params=params,
        cost_estimate=pl.CostEstimate(
            flops=3 * SLOTS * T**3, bytes_accessed=16 * 2**20, transcendentals=0
        ),
        name="prop_first",
    )(meta, *pieces, own, rec)
    return pl.pallas_call(
        second_kernel,
        in_specs=[smem] + [vmem] * 5,
        out_specs=[vmem] * 2,
        out_shape=[
            jax.ShapeDtypeStruct((ROWS, T), jnp.bfloat16),
            jax.ShapeDtypeStruct((ROWS, T), jnp.float32),
        ],
        scratch_shapes=[pltpu.VMEM(v.shape, v.dtype) for v in shapes[1:]],
        compiler_params=params,
        cost_estimate=pl.CostEstimate(
            flops=SLOTS * T**3, bytes_accessed=8 * 2**20, transcendentals=0
        ),
        name="prop_second",
    )(meta, swp_of, x_all, acc, norms, base)


def last_kernel(meta, *refs):
    pieces = refs[:14]
    own, rec, swp, inv, base, out, pack, x_all, acc = refs[14:]
    copy_pieces(pieces, x_all)
    acc[...] = jnp.zeros_like(acc)

    @pl.loop(0, 2)
    def _(i):
        add_tiles(own.at[pl.ds(i * 64, 64)], 64, i * 64, meta, x_all, acc)
        add_tiles(rec.at[pl.ds(i * 32, 32)], 32, SLOTS + i * 32, meta, x_all, acc)
        add_tiles(swp.at[pl.ds(i * 32, 32)], 32, SLOTS + SLOTS // 2 + i * 32, meta, x_all, acc)

    lane_half = lax.broadcasted_iota(jnp.int32, (T, T), 1) // HALF
    low, stay = lane_half == 0, lane_half != meta[6 * SLOTS]
    for r in range(RT // 2):
        done = []
        for k in (r, r + RT // 2):
            rows = slice(k * T, (k + 1) * T)
            done.append(base[rows] + inv[rows] * pair_sum(acc, k))
            out[rows] = done[-1].astype(jnp.bfloat16)
        same = jnp.where(low, done[0], done[1])
        moved = pltpu.roll(jnp.where(low, done[1], done[0]), HALF, 1)
        pack[r * T : (r + 1) * T] = jnp.where(stay, same, moved).astype(jnp.bfloat16)


def prop_last(meta, pieces, own, rec, swp, inv, base):
    vmem = pl.BlockSpec(memory_space=pltpu.VMEM)
    return pl.pallas_call(
        last_kernel,
        in_specs=[pl.BlockSpec(memory_space=pltpu.SMEM)] + [vmem] * 19,
        out_specs=[vmem] * 2,
        out_shape=[
            jax.ShapeDtypeStruct((ROWS, T), jnp.bfloat16),
            jax.ShapeDtypeStruct((ROWS // 2, T), jnp.bfloat16),
        ],
        scratch_shapes=[
            pltpu.VMEM((NZ * NY * ROWS, T), jnp.bfloat16),
            pltpu.VMEM((N_ACC, T, T), jnp.float32),
        ],
        compiler_params=pltpu.CompilerParams(vmem_limit_bytes=16 * 2**20),
        cost_estimate=pl.CostEstimate(
            flops=2 * 2 * SLOTS * T**3, bytes_accessed=16 * 2**20, transcendentals=0
        ),
        name="prop_last",
    )(meta, *pieces, own, rec, swp, inv, base)


def per_device(features, tile_values, tile_source, tile_target, tile_count, weights, bias_vector):
    blk, ch = lax.axis_index("blk"), lax.axis_index("ch")
    z, xh, y = blk // (NX * NY), (blk // NY) % NX, blk % NY
    xl, core = ch // 2, ch % 2

    swap_f = line_swap(features, 0, 0, 1)
    near = line_swap(features, 0, 1, 0)
    cross = line_swap(features, 1, 1, 0)
    over = line_swap(features, 1, 0, 0)
    swap_rest = [line_swap(v, 0, 0, 1) for v in (near, cross, over)]

    place = jnp.stack(
        [ch, xh, xl * 2 + core, (1 - xl) * 2 + core, xl * 2 + 1 - core, (1 - xl) * 2 + 1 - core]
    ).astype(jnp.int32)
    usable = jnp.arange(SLOTS, dtype=jnp.int32) < tile_count[0]
    source = jnp.where(usable, tile_source, 0)
    offset = source_rows(source, z, y)
    source_hi = (source // (RT * NY)) % NX
    slot = jnp.where(usable, (xh * 2 + source_hi) * RT + tile_target, DUMMY)
    norm_slot = jnp.where(usable, xh * RT + tile_target, 2 * RT)
    own_meta = jnp.stack([offset, slot, norm_slot]).astype(jnp.int32)
    far_meta = line_swap(own_meta, 1, 1, 0)
    far_meta = jnp.where(core == 0, far_meta, jnp.roll(far_meta, SLOTS // 2, axis=1))
    meta = jnp.concatenate([own_meta, far_meta], axis=1).reshape(-1)
    meta = jnp.concatenate([meta, xh.astype(jnp.int32)[None]])

    sent = lax.dynamic_slice_in_dim(tile_values, core * (SLOTS // 2), SLOTS // 2, 0)
    mask = jnp.arange(T, dtype=jnp.int32)[None, :] // HALF == xh

    received = line_swap(sent, 1, 1, 0)
    bias, meta, _, mask, place = lax.optimization_barrier((bias_vector, meta, sent, mask, place))
    u0, u1, u2 = mix(
        place, [features, near, cross, over, swap_f, *swap_rest], weights, bias[None, :]
    )

    rows_1 = gather_zy(u2)
    last_steps = (rows_1[7], rows_1[8], rows_1[12], rows_1[13])
    swapped = line_swap(after(received, last_steps), 0, 0, 1)
    v, inv_pair = prop_first(meta, rows_1, tile_values, received, swapped, u1)
    w, pack = prop_last(meta, gather_zy(v), tile_values, received, swapped, inv_pair, u0)
    back = line_swap(pack, 1, 0, 0)
    back = jnp.concatenate([back[:, :HALF], back[:, HALF:]], axis=0)
    back = jnp.concatenate([back, back], axis=1)
    return jnp.where(mask, w, back)


def solution(mesh):
    return jax.shard_map(
        per_device,
        mesh=mesh,
        in_specs=(P("blk", "ch"), P("blk", None, None), P("blk"), P("blk"), P("blk"), P(), P()),
        out_specs=P("blk", "ch"),
        check_vma=False,
    )
```
